128 devices in a mesh: basin: 16 (over x, y_lo, core), event: 8 (over z, y_hi).
Axes of the slice: x: 4, y: 4 (y_hi: 2, y_lo: 2; y = y_hi * 2 + y_lo), z: 4, core: 2. Of those that a mesh axis runs over, the one named last changes fastest.
Arguments:
- inputs: bfloat16 [8, 8, 6144, 256], P('event', None, 'basin'), may hold values from -6 to 6
- cotangent: bfloat16 [8, 6, 6144, 256], P('event', None, 'basin'), may hold values from -6 to 6
- conv_weight: bfloat16 [2, 256, 512], replicated, may hold values from -0.25 to 0.25
- conv_bias: float32 [512], replicated, may hold values from -4 to 4
- diffusion_weight: bfloat16 [5, 256, 256], replicated, may hold values from -0.15625 to 0.15625
- tiles_down: bfloat16 [48, 4, 128, 128], P('basin'), may hold values from -0.25 to 0.25
- tiles_up: bfloat16 [48, 4, 128, 128], P('basin'), may hold values from -0.25 to 0.25
- cols_down: int32 [48, 4], P('basin'), may hold values from 0 to 4, as said below
- cols_up: int32 [48, 4], P('basin'), may hold values from 0 to 4, as said below
- live_counts: int32 [16], P('basin'), may hold values from 192 to 384, as said below
Outputs:
- grad_inputs: bfloat16 [8, 8, 6144, 256], P('event', None, 'basin')
- grad_conv_weight: float32 [2, 256, 512], replicated
- grad_conv_bias: float32 [512], replicated
- grad_diffusion_weight: float32 [5, 256, 256], replicated
The draws below stay inside these ranges and needn't reach their ends.
Inputs may be any that keep to these rules, and one draw needn't show every extreme that they name: `cols_down`: in every row block, slot 0 names the block before it and slot 1 the block after it; the other slots name a block at most one away. A value v names the partition's own block v - 1 of its 3; 0 names the last block of the partition before, and 4 the first block of the partition after. `cols_up`: as for cols_down. `live_counts`: some partition is full and some holds exactly 192 live reaches in every draw.
All inputs are finite; a program needn't handle non-finite values.
Results may differ from the reference program's by a relative error of at most 0.008.
Values may be sent and summed in bfloat16 or wider, within the bound.
A program may use at most 128 MiB of HBM per device.

```python
import jax
import jax.numpy as jnp
from jax import lax

CHANNEL_COUNT = 256
TILE = 128
K = 4
T_IN = 8
DILATION_STEP = 2
R_DEV = 384
T_OUT = 6
EVENTS = 8
REACHES = 6144
NBLK = 48
BASINS = 16


def block_columns(key):
    blocks_dev = R_DEV // TILE
    offsets = jax.random.randint(key, (NBLK, K), -1, 2, dtype=jnp.int32)
    slot_ids = jnp.arange(K, dtype=jnp.int32)[None, :]
    offsets = jnp.where(slot_ids == 0, -1, jnp.where(slot_ids == 1, 1, offsets))
    local_block = (jnp.arange(NBLK, dtype=jnp.int32) % blocks_dev)[:, None]
    return (local_block + 1 + offsets).astype(jnp.int32)


def draw_cols_down(key, part):
    key = jax.random.fold_in(key, 11)
    return block_columns(key)


def draw_cols_up(key, part):
    key = jax.random.fold_in(key, 23)
    return block_columns(key)


def draw_live_counts(key, part):
    key = jax.random.fold_in(key, 37)
    key_counts, key_order = jax.random.split(key)
    counts = jax.random.randint(key_counts, (BASINS,), R_DEV // 2, R_DEV + 1, dtype=jnp.int32)
    chosen = jax.random.permutation(key_order, BASINS)
    counts = counts.at[chosen[0]].set(R_DEV).at[chosen[1]].set(R_DEV // 2)
    return counts.astype(jnp.int32)


def level_of(key, shape, cuts, smallest, top_value):
    level, own = 1.0, jax.random.fold_in(key, 6)
    for axis_at, parts in cuts:
        steps = jnp.exp(jax.random.uniform(jax.random.fold_in(own, axis_at), (parts,), jnp.float32, smallest / len(cuts), top_value / len(cuts)))
        level = level * jnp.repeat(steps, shape[axis_at] // parts).reshape([-1 if axis == axis_at else 1 for axis in range(len(shape))])
    return level


def scatter_about(rng, shape, spread, most, cuts=(), kind=jnp.bfloat16):
    entries = spread * jax.random.normal(rng, shape, jnp.float32)
    if cuts:
        entries = entries * level_of(rng, shape, cuts, -0.22, 0.18)
    return jnp.clip(entries, -most, most).astype(kind)


def setup_inputs(seed: int = 0) -> dict:
    splits = jax.random.split(jax.random.key(seed), 11)
    inputs = scatter_about(splits[0], (EVENTS, T_IN, REACHES, CHANNEL_COUNT), 1.0, 6.0, ((0, 8), (2, 16)))
    cotangent = scatter_about(splits[1], (EVENTS, T_OUT, REACHES, CHANNEL_COUNT), 1.0, 6.0, ((0, 8), (2, 16)))
    conv_weight = scatter_about(splits[2], (2, CHANNEL_COUNT, 2 * CHANNEL_COUNT), (2 * CHANNEL_COUNT) ** -0.5, 0.25)
    conv_bias = scatter_about(splits[3], (2 * CHANNEL_COUNT,), 1.0, 4.0, (), jnp.float32)
    diffusion_weight = scatter_about(splits[4], (5, CHANNEL_COUNT, CHANNEL_COUNT), (5 * CHANNEL_COUNT) ** -0.5, 0.15625)
    tiles_down = scatter_about(splits[5], (NBLK, K, TILE, TILE), (K * TILE) ** -0.5, 0.25, ((0, 16),))
    tiles_up = scatter_about(splits[6], (NBLK, K, TILE, TILE), (K * TILE) ** -0.5, 0.25, ((0, 16),))
    cols_down = draw_cols_down(jax.random.fold_in(splits[10], 71), 0)
    cols_up = draw_cols_up(jax.random.fold_in(splits[10], 71), 0)
    live_counts = draw_live_counts(jax.random.fold_in(splits[10], 71), 0)
    return dict(inputs=inputs, cotangent=cotangent, conv_weight=conv_weight, conv_bias=conv_bias, diffusion_weight=diffusion_weight, tiles_down=tiles_down, tiles_up=tiles_up, cols_down=cols_down, cols_up=cols_up, live_counts=live_counts)


def live_rows(live_counts):
    reach_ids = jnp.arange(REACHES, dtype=jnp.int32)
    local_ids = reach_ids % R_DEV
    owner_ids = reach_ids // R_DEV
    count_of = live_counts[owner_ids]
    live_flag = (local_ids < count_of - TILE) | (local_ids >= R_DEV - TILE)
    return live_flag.astype(jnp.float32)


def global_blocks(col_set):
    per_dev = R_DEV // TILE
    row_block = jnp.arange(NBLK, dtype=jnp.int32)[:, None]
    target = (row_block // per_dev) * per_dev + col_set - 1
    in_range = ((target >= 0) & (target < NBLK)).astype(jnp.float32)
    return jnp.clip(target, 0, NBLK - 1).astype(jnp.int32), in_range


def apply_tiles(tile_set, target, in_range, source):
    summed = jnp.zeros(source.shape, jnp.float32)
    for slot_idx in range(K):
        picked = jnp.take(source, target[:, slot_idx], axis=1).astype(jnp.float32)
        weighted = tile_set[:, slot_idx].astype(jnp.float32) * in_range[:, slot_idx][:, None, None]
        summed = summed + jnp.einsum("bpq,tbqc->tbpc", weighted, picked)
    return summed


def apply_transposed(tile_set, target, in_range, source):
    summed = jnp.zeros(source.shape, jnp.float32)
    for slot_idx in range(K):
        weighted = tile_set[:, slot_idx].astype(jnp.float32) * in_range[:, slot_idx][:, None, None]
        product = jnp.einsum("bpq,tbpc->tbqc", weighted, source.astype(jnp.float32))
        gathered_sum = jax.ops.segment_sum(jnp.moveaxis(product, 1, 0), target[:, slot_idx], num_segments=NBLK)
        summed = summed + jnp.moveaxis(gathered_sum, 0, 1)
    return summed


def reference(inputs, cotangent, conv_weight, conv_bias, diffusion_weight, tiles_down, tiles_up, cols_down, cols_up, live_counts):
    live_flag = live_rows(live_counts)
    row_mask = jnp.tile(live_flag, T_OUT)[:, None]
    block_mask = live_flag.reshape(1, NBLK, TILE, 1)
    down_target, down_range = global_blocks(cols_down)
    up_target, up_range = global_blocks(cols_up)
    grad_scale = float(EVENTS * T_OUT * REACHES) ** -0.5

    def one_event(running, event_pair):
        event_input, event_cot = event_pair
        first_tap = event_input[:T_OUT].reshape(-1, CHANNEL_COUNT)
        later_tap = event_input[DILATION_STEP:].reshape(-1, CHANNEL_COUNT)
        pre_act = (jnp.dot(first_tap, conv_weight[0], preferred_element_type=jnp.float32)
                   + jnp.dot(later_tap, conv_weight[1], preferred_element_type=jnp.float32) + conv_bias)
        filter_act = jnp.tanh(pre_act[:, :CHANNEL_COUNT])
        gate_act = jax.nn.sigmoid(pre_act[:, CHANNEL_COUNT:])
        hidden = (filter_act * gate_act * row_mask).astype(jnp.bfloat16)
        hidden_blocks = hidden.reshape(T_OUT, NBLK, TILE, CHANNEL_COUNT)
        down_one = (apply_tiles(tiles_down, down_target, down_range, hidden_blocks) * block_mask).astype(jnp.bfloat16)
        down_two = (apply_tiles(tiles_down, down_target, down_range, down_one) * block_mask).astype(jnp.bfloat16)
        up_one = (apply_tiles(tiles_up, up_target, up_range, hidden_blocks) * block_mask).astype(jnp.bfloat16)
        up_two = (apply_tiles(tiles_up, up_target, up_range, up_one) * block_mask).astype(jnp.bfloat16)
        gated_cot = event_cot * live_flag.astype(jnp.bfloat16)[None, :, None]
        gated_flat = gated_cot.reshape(-1, CHANNEL_COUNT)
        features = [hidden_blocks, down_one, down_two, up_one, up_two]
        diff_grads = jnp.stack([jnp.dot(feature.reshape(-1, CHANNEL_COUNT).T, gated_flat, preferred_element_type=jnp.float32) for feature in features])
        cot_parts = [jnp.dot(gated_flat, diffusion_weight[weight_idx].T, preferred_element_type=jnp.float32).astype(jnp.bfloat16).reshape(T_OUT, NBLK, TILE, CHANNEL_COUNT) for weight_idx in range(5)]
        cot_down = ((cot_parts[1].astype(jnp.float32) + apply_transposed(tiles_down, down_target, down_range, cot_parts[2])) * block_mask).astype(jnp.bfloat16)
        cot_up = ((cot_parts[3].astype(jnp.float32) + apply_transposed(tiles_up, up_target, up_range, cot_parts[4])) * block_mask).astype(jnp.bfloat16)
        grad_hidden = (cot_parts[0].astype(jnp.float32)
                       + apply_transposed(tiles_down, down_target, down_range, cot_down)
                       + apply_transposed(tiles_up, up_target, up_range, cot_up)).reshape(-1, CHANNEL_COUNT) * row_mask
        grad_filter = grad_hidden * gate_act * (1.0 - filter_act * filter_act)
        grad_gate = grad_hidden * filter_act * gate_act * (1.0 - gate_act)
        grad_pre = jnp.concatenate([grad_filter, grad_gate], axis=1).astype(jnp.bfloat16)
        conv_grads = jnp.stack([jnp.dot(first_tap.T, grad_pre, preferred_element_type=jnp.float32),
                                jnp.dot(later_tap.T, grad_pre, preferred_element_type=jnp.float32)])
        bias_grads = jnp.sum(grad_pre.astype(jnp.float32), axis=0)
        backward_first_hop = jnp.dot(grad_pre, conv_weight[0].T, preferred_element_type=jnp.float32).reshape(T_OUT, REACHES, CHANNEL_COUNT)
        backward_second_hop = jnp.dot(grad_pre, conv_weight[1].T, preferred_element_type=jnp.float32).reshape(T_OUT, REACHES, CHANNEL_COUNT) + gated_cot.astype(jnp.float32)
        input_gradient = (jnp.pad(backward_first_hop, ((0, DILATION_STEP), (0, 0), (0, 0))) + jnp.pad(backward_second_hop, ((DILATION_STEP, 0), (0, 0), (0, 0)))).astype(jnp.bfloat16)
        running = (running[0] + conv_grads, running[1] + bias_grads, running[2] + diff_grads)
        return running, input_gradient

    initial = (jnp.zeros((2, CHANNEL_COUNT, 2 * CHANNEL_COUNT), jnp.float32), jnp.zeros((2 * CHANNEL_COUNT,), jnp.float32), jnp.zeros((5, CHANNEL_COUNT, CHANNEL_COUNT), jnp.float32))
    totals, grad_inputs = lax.scan(one_event, initial, (inputs, cotangent))
    return grad_inputs, totals[0] * grad_scale, totals[1] * grad_scale, totals[2] * grad_scale
```

```python
import functools

import jax
import jax.numpy as jnp
from jax import lax
from jax.experimental import pallas as pl
from jax.experimental.pallas import tpu as pltpu
from jax.sharding import PartitionSpec as P

MESH = pl.DeviceIdType.MESH
BF = jnp.bfloat16
F32 = jnp.float32
T_IN, T_OUT, STEP = 8, 6, 2
ROWS, CH, TILE, NB = 384, 256, 128, 3
EXT = ROWS + 4 * TILE
MATS = 10
GROUPS = (
    (0, 3, ("x", "z", "y")),
    (3, 3, ("z", "y", "x")),
    (6, 4, ("y", "x", "z")),
)


def dot(a, b):
    return jnp.dot(a, b, preferred_element_type=F32)


def place():
    b, e = lax.axis_index("basin"), lax.axis_index("event")
    pos = {"x": b // 4, "y": (e % 2) * 2 + (b // 2) % 2, "z": e // 2}
    return b, e, b % 2, pos


def peer(core, pos, axis, q):
    at = dict(pos)
    at[axis] = q
    x, y, z = at["x"], at["y"], at["z"]
    return ((x * 2 + y % 2) * 2 + core, z * 2 + y // 2)


def remote(src, dst, send, recv, to):
    return pltpu.make_async_remote_copy(
        src_ref=src, dst_ref=dst, send_sem=send, recv_sem=recv, device_id=to, device_id_type=MESH
    )


def rows_at(index, size):
    return pl.ds(pl.multiple_of(index * size, size), size)


def all_reduce(half_of, core, pos, sib, bufs, sems, beside):
    s0, r0, s1, whole, r1s, s2s, r2s, r3s, s4s = bufs
    c_send, c_recv, send, recv = sems
    for m in range(MATS):
        for c in range(2):
            s0[m, c] = half_of(m, c, 1 - core).astype(BF)
    first = remote(s0, r0, c_send.at[0], c_recv.at[0], sib)
    first.start()
    beside(0)
    first.wait()
    for m in range(MATS):
        for c in range(2):
            s1[m, c] = (half_of(m, c, core) + r0[m, c].astype(F32)).astype(BF)

    def exchange(stage, src_of, dst_of, in_of, axis_of):
        copies = []
        for g, (lo, n, axes) in enumerate(GROUPS):
            axis = axes[axis_of]
            a = pos[axis]
            for k in (1, 2, 3):
                q = (a + k) % 4
                args = (send.at[stage, g, k - 1], recv.at[stage, g, k - 1], peer(core, pos, axis, q))
                out = remote(src_of(g, q), dst_of(g, k, a), *args)
                out.start()
                back = remote(src_of(g, q), in_of(g, k, (a + 4 - k) % 4), *args)
                copies.append((g, out, back))
        return copies

    def finish(copies, g):
        for h, out, back in copies:
            if h == g:
                back.wait_recv()
                out.wait_send()

    r1_at = lambda g, k, a: r1s[g].at[k - 1]
    copies = exchange(
        0,
        lambda g, q: s1.at[GROUPS[g][0] : GROUPS[g][0] + GROUPS[g][1], :, rows_at(q, 32), :],
        r1_at,
        r1_at,
        0,
    )
    beside(1)
    for g, (lo, n, axes) in enumerate(GROUPS):
        finish(copies, g)
        total = s1[lo : lo + n, :, rows_at(pos[axes[0]], 32), :].astype(F32)
        for k in range(3):
            total = total + r1s[g][k].astype(F32)
        for half in range(2):
            for c in range(2):
                s2s[g][2 * half + c] = total[:, c, half * 16 : half * 16 + 16, :].astype(BF)
    r2_at = lambda g, k, a: r2s[g].at[k - 1]
    copies = exchange(1, lambda g, q: s2s[g].at[q], r2_at, r2_at, 1)
    beside(2)
    for g, (lo, n, axes) in enumerate(GROUPS):
        finish(copies, g)
        total = s2s[g][pos[axes[1]]].astype(F32)
        for k in range(3):
            total = total + r2s[g][k].astype(F32)
        r3s[g][pos[axes[2]]] = total.astype(BF)
    copies = exchange(
        2,
        lambda g, q: r3s[g].at[pos[GROUPS[g][2][2]]],
        lambda g, k, a: r3s[g].at[a],
        lambda g, k, a: r3s[g].at[a],
        2,
    )
    beside(3)

    def spot(g, a):
        lo, n, axes = GROUPS[g]
        row = pl.ds(pl.multiple_of(pos[axes[0]] * 32 + (a // 2) * 16, 16), 16)
        return whole.at[core, lo : lo + n, a % 2, row, :]

    for g, (lo, n, axes) in enumerate(GROUPS):
        finish(copies, g)
        total = r3s[g][0].astype(F32)
        for k in range(1, 4):
            total = total + r3s[g][k].astype(F32)
        a = pos[axes[1]]
        row = pl.ds(pl.multiple_of(pos[axes[0]] * 32 + (a // 2) * 16, 16), 16)
        whole[core, lo : lo + n, a % 2, row, :] = total.astype(BF)
    copies = exchange(
        3,
        lambda g, q: spot(g, pos[GROUPS[g][2][1]]),
        lambda g, k, a: spot(g, a),
        lambda g, k, a: spot(g, a),
        1,
    )
    beside(4)

    def band(g, a):
        lo, n, axes = GROUPS[g]
        return whole.at[core, lo : lo + n, :, rows_at(a, 32), :]

    for g in range(len(GROUPS)):
        finish(copies, g)
    copies = exchange(
        4,
        lambda g, q: band(g, pos[GROUPS[g][2][0]]),
        lambda g, k, a: band(g, a),
        lambda g, k, a: band(g, a),
        0,
    )
    beside(5)
    last = []
    for g, (lo, n, axes) in enumerate(GROUPS):
        finish(copies, g)
        args = (c_send.at[1 + g], c_recv.at[1 + g], sib)
        out = remote(whole.at[core, lo : lo + n], whole.at[core, lo : lo + n], *args)
        out.start()
        last.append((out, remote(whole.at[core, lo : lo + n], whole.at[1 - core, lo : lo + n], *args)))
    beside(6)
    for out, back in last:
        back.wait_recv()
        out.wait_send()


def ar_scratch():
    n = len(GROUPS)
    bufs = [
        pltpu.VMEM((MATS, 2, TILE, TILE), BF),
        pltpu.VMEM((MATS, 2, TILE, TILE), BF),
        pltpu.VMEM((MATS, 2, TILE, TILE), BF),
        pltpu.VMEM((2, MATS, 2, TILE, TILE), BF),
    ]
    bufs += [pltpu.VMEM((3, g[1], 2, 32, TILE), BF) for g in GROUPS]
    bufs += [pltpu.VMEM((4, g[1], 16, TILE), BF) for g in GROUPS]
    bufs += [pltpu.VMEM((3, g[1], 16, TILE), BF) for g in GROUPS]
    bufs += [pltpu.VMEM((4, g[1], 16, TILE), BF) for g in GROUPS]
    sems = [
        pltpu.SemaphoreType.DMA((1 + n,)),
        pltpu.SemaphoreType.DMA((1 + n,)),
        pltpu.SemaphoreType.DMA((5, n, 3)),
        pltpu.SemaphoreType.DMA((5, n, 3)),
    ]
    return bufs, sems


def split_ar(refs):
    n = len(GROUPS)
    bufs = (*refs[:4], refs[4 : 4 + n], refs[4 + n : 4 + 2 * n], refs[4 + 2 * n : 4 + 3 * n], refs[4 + 3 * n : 4 + 4 * n], None)
    return bufs, refs[4 + 4 * n :]


def body(
    scale, x_in, cot_in, cw_in, cb_in, dw_in, td_in, tu_in, cd_in, cu_in, live_in,
    gi_out, gc_out, gb_out, gd_out,
    xs, cext, cw, cb, dw, tiles, vown, send_l, send_r, recv_l, recv_r, big, mask,
    wcat, cwt, ht, xt, ab, feats, gps, gacc, cacc, bacc,
    load_sem, tile_send, tile_recv, halo_send, halo_recv, *ar_refs,
):
    b, e, core, pos = place()
    right, left = ((b + 1) % 16, e), ((b + 15) % 16, e)
    sib = (b + 1 - 2 * core, e)
    barrier = pltpu.get_barrier_semaphore()
    greeted = [left, right] + [
        peer(core, pos, axis, (pos[axis] + k) % 4) for axis in ("x", "y", "z") for k in (1, 2, 3)
    ]
    for to in greeted:
        pl.semaphore_signal(barrier, inc=1, device_id=to, device_id_type=MESH)
    loads = [
        pltpu.make_async_copy(src, dst, load_sem.at[i])
        for i, (src, dst) in enumerate(
            [
                (td_in, tiles.at[0]),
                (tu_in, tiles.at[1]),
                (x_in, xs),
                (cw_in, cw),
                (cb_in, cb),
                (cot_in, cext.at[:, 2 * TILE : 2 * TILE + ROWS, :]),
                (dw_in, dw),
            ]
        )
    ]
    for load in loads:
        load.start()

    live = live_in[0]
    reach = lax.broadcasted_iota(jnp.int32, (ROWS, CH), 0)
    mask[...] = jnp.where((reach < live - TILE) | (reach >= ROWS - TILE), 1.0, 0.0).astype(F32)
    loads[0].wait()
    loads[1].wait()
    for way, cols in enumerate((cd_in, cu_in)):
        for r in range(NB):
            keep = mask[r * TILE : (r + 1) * TILE, :TILE]
            slots = [tiles[way, r, k].astype(F32) for k in range(4)]
            for o in range(3):
                total = jnp.zeros((TILE, TILE), F32)
                if o == 0:
                    total = total + slots[0]
                if o == 2:
                    total = total + slots[1]
                for k in (2, 3):
                    total = total + jnp.where(cols[r, k] - r == o, 1.0, 0.0).astype(F32) * slots[k]
                total = total * keep
                if r == 0 and o == 0:
                    total = total * jnp.where(b > 0, 1.0, 0.0).astype(F32)
                if r == NB - 1 and o == 2:
                    total = total * jnp.where(b < 15, 1.0, 0.0).astype(F32)
                tile = total.T.astype(BF)
                vown[way, r, o] = tile
                if (r, o) in ((1, 2), (2, 1), (2, 2)):
                    send_r[way, ((1, 2), (2, 1), (2, 2)).index((r, o))] = tile
                if (r, o) in ((0, 0), (0, 1), (1, 0)):
                    send_l[way, ((0, 0), (0, 1), (1, 0)).index((r, o))] = tile

    pl.semaphore_wait(barrier, len(greeted))
    tile_copies = [
        remote(send_r, recv_l, tile_send.at[0], tile_recv.at[0], right),
        remote(send_l, recv_r, tile_send.at[1], tile_recv.at[1], left),
    ]
    for copy in tile_copies:
        copy.start()

    def halo(t):
        return [
            remote(
                cot_in.at[t, TILE:ROWS, :], cext.at[t, 0 : 2 * TILE, :],
                halo_send.at[t, 0], halo_recv.at[t, 0], right,
            ),
            remote(
                cot_in.at[t, 0 : 2 * TILE, :], cext.at[t, 2 * TILE + ROWS : EXT, :],
                halo_send.at[t, 1], halo_recv.at[t, 1], left,
            ),
        ]

    @pl.loop(0, T_OUT)
    def _(t):
        for copy in halo(t):
            copy.start()

    for load in loads[2:]:
        load.wait()

    @pl.loop(0, T_OUT)
    def _(t):
        pre = dot(xs[t], cw[0]) + dot(xs[t + STEP], cw[1]) + cb[...]
        f = jnp.tanh(pre[:, :CH])
        s = 0.5 * jnp.tanh(0.5 * pre[:, CH:]) + 0.5
        sm = s * mask[...]
        fs = f * sm
        ht[t] = fs.astype(BF).T
        ab[t, :, :CH] = sm * (1.0 - f * f)
        ab[t, :, CH:] = fs * (1.0 - s)

    @pl.loop(0, T_IN)
    def _(t):
        xt[t] = xs[t].T

    for k in range(5):
        wcat[k * CH : (k + 1) * CH, :] = dw[k].T
    for k in range(2):
        cwt[k] = cw[k].T
    gps[0:STEP] = jnp.zeros((STEP, ROWS, 2 * CH), BF)
    gacc[...] = jnp.zeros_like(gacc)
    cacc[...] = jnp.zeros_like(cacc)
    bacc[...] = jnp.zeros_like(bacc)

    for copy in tile_copies:
        copy.wait()

    def v(way, i, k):
        if 0 <= i < NB:
            return vown[way, i, k - i + 1]
        if i < 0:
            return recv_l[way, ((-2, -1), (-1, -1), (-1, 0)).index((i, k))]
        return recv_r[way, ((3, 2), (3, 3), (4, 3)).index((i, k))]

    for j in range(NB):
        for way in range(2):
            for at, i in enumerate(range(j - 2, j + 3)):
                total = jnp.zeros((TILE, TILE), F32)
                for k in range(j - 1, j + 2):
                    if abs(i - k) <= 1:
                        total = total + dot(v(way, k, j), v(way, i, k))
                first = v(way, i, j) if abs(i - j) <= 1 else jnp.zeros((TILE, TILE), BF)
                big[j, way * TILE : (way + 1) * TILE, at * TILE : (at + 1) * TILE] = first
                big[j, (2 + way) * TILE : (3 + way) * TILE, at * TILE : (at + 1) * TILE] = total.astype(BF)

    @pl.loop(0, T_OUT)
    def _(t):
        for copy in halo(t):
            copy.wait()
        feats[:, :CH] = cext[t, 2 * TILE : 2 * TILE + ROWS, :]
        for j in range(NB):
            out = dot(big[j], cext[t, j * TILE : (j + 5) * TILE, :]).astype(BF)
            for at, k in enumerate((1, 3, 2, 4)):
                feats[j * TILE : (j + 1) * TILE, k * CH : (k + 1) * CH] = out[at * TILE : (at + 1) * TILE]
        gacc[...] += dot(ht[t], feats[...])
        gh = dot(feats[...], wcat[...])
        ga = gh * ab[t, :, :CH]
        gb = gh * ab[t, :, CH:]
        gp = jnp.concatenate([ga, gb], axis=1).astype(BF)
        gps[t + STEP] = gp
        cacc[0] += dot(xt[t], gp)
        cacc[1] += dot(xt[t + STEP], gp)
        bacc[...] += jnp.sum(gp.astype(F32).reshape(ROWS // 8, 8, 2 * CH), axis=0)
        before = jnp.maximum(t - STEP, 0)
        own = cext[before, 2 * TILE : 2 * TILE + ROWS, :].astype(F32) * mask[...]
        own = own * jnp.where(t >= STEP, 1.0, 0.0).astype(F32)
        gi_out[t] = (dot(gp, cwt[0]) + dot(gps[t], cwt[1]) + own).astype(BF)

    line = jnp.sum(bacc[...], axis=0, keepdims=True)
    row = lax.broadcasted_iota(jnp.int32, (16, TILE), 0)
    bias = jnp.zeros((16, TILE), F32)
    for i in range(4):
        bias = bias + jnp.where(row == i, jnp.broadcast_to(line[:, i * TILE : (i + 1) * TILE], (16, TILE)), 0.0)
    bias = jnp.broadcast_to(bias[None], (TILE // 16, 16, TILE)).reshape(TILE, TILE)

    def half_of(m, c, half):
        if m < 5:
            return gacc[rows_at(half, TILE), m * CH + c * TILE : m * CH + (c + 1) * TILE]
        if m < 9:
            at = ((m - 5) % 2) * CH + c * TILE
            return cacc[(m - 5) // 2, rows_at(half, TILE), at : at + TILE]
        return bias

    def beside(stage):
        if stage < STEP:
            t = T_OUT + stage
            own = cext[t - STEP, 2 * TILE : 2 * TILE + ROWS, :].astype(F32) * mask[...]
            gi_out[t] = (dot(gps[t], cwt[1]) + own).astype(BF)

    bufs, sems = split_ar(ar_refs)
    all_reduce(half_of, core, pos, sib, bufs, sems, beside)
    whole = bufs[3]
    for h in range(2):
        for c in range(2):
            rows = slice(h * TILE, (h + 1) * TILE)
            for m in range(9):
                part = whole[h, m, c].astype(F32) * scale
                if m < 5:
                    gd_out[m, rows, c * TILE : (c + 1) * TILE] = part
                else:
                    at = ((m - 5) % 2) * CH + c * TILE
                    gc_out[(m - 5) // 2, rows, at : at + TILE] = part
    gb_out[...] = whole[0, 9, 0, 0:16, :].astype(F32) * scale


def on_device(x, cot, cw, cb, dw, td, tu, cd, cu, live):
    scale = float(8 * T_OUT * 6144) ** (-0.5)
    bufs, sems = ar_scratch()
    anywhere = pl.BlockSpec(memory_space=pl.ANY)
    vmem = pl.BlockSpec(memory_space=pltpu.VMEM)
    smem = pl.BlockSpec(memory_space=pltpu.SMEM)
    gi, gc, gb, gd = pl.pallas_call(
        functools.partial(body, scale),
        out_shape=(
            jax.ShapeDtypeStruct((T_IN, ROWS, CH), BF),
            jax.ShapeDtypeStruct((2, CH, 2 * CH), F32),
            jax.ShapeDtypeStruct((16, TILE), F32),
            jax.ShapeDtypeStruct((5, CH, CH), F32),
        ),
        in_specs=[anywhere] * 7 + [smem] * 3,
        out_specs=(vmem,) * 4,
        scratch_shapes=[
            pltpu.VMEM((T_IN, ROWS, CH), BF),
            pltpu.VMEM((T_OUT, EXT, CH), BF),
            pltpu.VMEM((2, CH, 2 * CH), BF),
            pltpu.VMEM((1, 2 * CH), F32),
            pltpu.VMEM((5, CH, CH), BF),
            pltpu.VMEM((2, NB, 4, TILE, TILE), BF),
            pltpu.VMEM((2, NB, 3, TILE, TILE), BF),
            pltpu.VMEM((2, 3, TILE, TILE), BF),
            pltpu.VMEM((2, 3, TILE, TILE), BF),
            pltpu.VMEM((2, 3, TILE, TILE), BF),
            pltpu.VMEM((2, 3, TILE, TILE), BF),
            pltpu.VMEM((NB, 4 * TILE, 5 * TILE), BF),
            pltpu.VMEM((ROWS, CH), F32),
            pltpu.VMEM((5 * CH, CH), BF),
            pltpu.VMEM((2, 2 * CH, CH), BF),
            pltpu.VMEM((T_OUT, CH, ROWS), BF),
            pltpu.VMEM((T_IN, CH, ROWS), BF),
            pltpu.VMEM((T_OUT, ROWS, 2 * CH), F32),
            pltpu.VMEM((ROWS, 5 * CH), BF),
            pltpu.VMEM((T_IN, ROWS, 2 * CH), BF),
            pltpu.VMEM((CH, 5 * CH), F32),
            pltpu.VMEM((2, CH, 2 * CH), F32),
            pltpu.VMEM((8, 2 * CH), F32),
            pltpu.SemaphoreType.DMA((7,)),
            pltpu.SemaphoreType.DMA((2,)),
            pltpu.SemaphoreType.DMA((2,)),
            pltpu.SemaphoreType.DMA((T_OUT, 2)),
            pltpu.SemaphoreType.DMA((T_OUT, 2)),
            *bufs,
            *sems,
        ],
        compiler_params=pltpu.CompilerParams(
            collective_id=0, has_side_effects=True, vmem_limit_bytes=56 << 20
        ),
    )(x[0], cot[0], cw, cb.reshape(1, -1), dw, td, tu, cd, cu, live)
    return gi[None], gc, gb[0:4].reshape(-1), gd


def solution(mesh):
    return jax.shard_map(
        on_device,
        mesh=mesh,
        in_specs=(
            P("event", None, "basin", None),
            P("event", None, "basin", None),
            P(),
            P(),
            P(),
            P("basin", None, None, None),
            P("basin", None, None, None),
            P("basin", None),
            P("basin", None),
            P("basin"),
        ),
        out_specs=(P("event", None, "basin", None), P(), P(), P()),
        check_vma=False,
    )
```

```python
import functools

import jax
import jax.numpy as jnp
from jax import lax
from jax.experimental import pallas as pl
from jax.experimental.pallas import tpu as pltpu
from jax.sharding import PartitionSpec as P

MESH = pl.DeviceIdType.MESH
BF = jnp.bfloat16
F32 = jnp.float32
T_IN, T_OUT, STEP = 8, 6, 2
ROWS, CH, TILE, NB = 384, 256, 128, 3
EXT = ROWS + 4 * TILE
MATS = 10
GROUPS = (
    (0, 3, ("x", "z", "y")),
    (3, 3, ("z", "y", "x")),
    (6, 4, ("y", "x", "z")),
)


def dot(a, b):
    return jnp.dot(a, b, preferred_element_type=F32)


def place():
    b, e = lax.axis_index("basin"), lax.axis_index("event")
    pos = {"x": b // 4, "y": (e % 2) * 2 + (b // 2) % 2, "z": e // 2}
    return b, e, b % 2, pos


def peer(core, pos, moved):
    x, y, z = ({**pos, **moved}[axis] for axis in ("x", "y", "z"))
    return ((x * 2 + y % 2) * 2 + core, z * 2 + y // 2)


def remote(src, dst, send, recv, to):
    return pltpu.make_async_remote_copy(
        src_ref=src, dst_ref=dst, send_sem=send, recv_sem=recv, device_id=to, device_id_type=MESH
    )


def rows_at(index, size):
    return pl.ds(pl.multiple_of(index * size, size), size)


class AllReduce:
    def __init__(self, half_of, core, pos, sib, bufs, sems):
        self.half_of, self.core, self.pos, self.sib = half_of, core, pos, sib
        self.s0, self.r0, self.s1, self.whole, self.r1s, self.s2s, self.r2s, self.r3s = bufs
        self.c_send, self.c_recv, self.send, self.recv = sems
        self.flying = {}

    def core_send(self, g):
        lo, n, _ = GROUPS[g]
        for m in range(lo, lo + n):
            for c in range(2):
                self.s0[m, c] = self.half_of(m, c, 1 - self.core).astype(BF)
        mats = pl.ds(lo, n)
        copy = remote(self.s0.at[mats], self.r0.at[mats], self.c_send.at[0, g], self.c_recv.at[0, g], self.sib)
        copy.start()
        self.flying["core", g] = copy

    def exchange(self, stage, g, src_of, dst_of, in_of, axis):
        a = self.pos[axis]
        copies = []
        for k in (1, 2, 3):
            q = (a + k) % 4
            args = (self.send.at[stage, g, k - 1], self.recv.at[stage, g, k - 1], peer(self.core, self.pos, {axis: q}))
            out = remote(src_of(q), dst_of(k, a), *args)
            out.start()
            copies.append((out, remote(src_of(q), in_of(k, (a + 4 - k) % 4), *args)))
        self.flying[stage, g] = copies

    def finish(self, stage, g):
        for out, back in self.flying[stage, g]:
            back.wait_recv()

    def scatter_first(self, g):
        lo, n, axes = GROUPS[g]
        self.flying["core", g].wait()
        for m in range(lo, lo + n):
            for c in range(2):
                self.s1[m, c] = (self.half_of(m, c, self.core) + self.r0[m, c].astype(F32)).astype(BF)
        dst = lambda k, a: self.r1s[g].at[k - 1]
        self.exchange(0, g, lambda q: self.s1.at[lo : lo + n, :, rows_at(q, 32), :], dst, dst, axes[0])

    def scatter_second(self, g):
        lo, n, axes = GROUPS[g]
        self.finish(0, g)
        total = self.s1[lo : lo + n, :, rows_at(self.pos[axes[0]], 32), :].astype(F32)
        for k in range(3):
            total = total + self.r1s[g][k].astype(F32)
        for half in range(2):
            for c in range(2):
                self.s2s[g][2 * half + c] = total[:, c, half * 16 : half * 16 + 16, :]
        dst = lambda k, a: self.r2s[g].at[k - 1]
        self.exchange(1, g, lambda q: self.s2s[g].at[q], dst, dst, axes[1])

    def sum_third(self, g):
        lo, n, axes = GROUPS[g]
        self.finish(1, g)
        total = self.s2s[g][self.pos[axes[1]]]
        for k in range(3):
            total = total + self.r2s[g][k]
        a = self.pos[axes[2]]
        self.r3s[g][a] = total
        dst = lambda k, a: self.r3s[g].at[a]
        self.exchange(2, g, lambda q: self.r3s[g].at[a], dst, dst, axes[2])

    def spot(self, g, a):
        lo, n, axes = GROUPS[g]
        row = pl.ds(pl.multiple_of(self.pos[axes[0]] * 32 + (a // 2) * 16, 16), 16)
        return self.core, pl.ds(lo, n), a % 2, row, slice(None)

    def gather_second(self, g):
        lo, n, axes = GROUPS[g]
        self.finish(2, g)
        total = self.r3s[g][0]
        for k in range(1, 4):
            total = total + self.r3s[g][k]
        a = self.pos[axes[1]]
        self.whole[self.spot(g, a)] = total.astype(BF)
        dst = lambda k, a: self.whole.at[self.spot(g, a)]
        self.exchange(3, g, lambda q: self.whole.at[self.spot(g, a)], dst, dst, axes[1])

    def band(self, g, a, core):
        lo, n, axes = GROUPS[g]
        return self.whole.at[core, lo : lo + n, :, rows_at(a, 32), :]

    def to_core(self, g, i, a):
        args = (self.c_send.at[1 + i, g], self.c_recv.at[1 + i, g], self.sib)
        out = remote(self.band(g, a, self.core), self.band(g, a, self.core), *args)
        out.start()
        self.flying["back", g, i] = (out, remote(self.band(g, a, self.core), self.band(g, a, 1 - self.core), *args))

    def gather_first(self, g):
        axes = GROUPS[g][2]
        self.finish(3, g)
        a = self.pos[axes[0]]
        dst = lambda k, a: self.band(g, a, self.core)
        self.exchange(4, g, lambda q: self.band(g, a, self.core), dst, dst, axes[0])
        self.to_core(g, 0, a)

    def gather_core(self, g):
        a = self.pos[GROUPS[g][2][0]]
        for i, (out, back) in enumerate(self.flying[4, g]):
            back.wait_recv()
            self.to_core(g, 1 + i, (a + 3 - i) % 4)

    def end(self, g):
        for i in range(4):
            out, back = self.flying["back", g, i]
            back.wait_recv()

    def drain(self, g):
        for stage in range(5):
            for out, back in self.flying[stage, g]:
                out.wait_send()
        for i in range(4):
            self.flying["back", g, i][0].wait_send()


def ar_scratch():
    n = len(GROUPS)
    bufs = [
        pltpu.VMEM((MATS, 2, TILE, TILE), BF),
        pltpu.VMEM((MATS, 2, TILE, TILE), BF),
        pltpu.VMEM((MATS, 2, TILE, TILE), BF),
        pltpu.VMEM((2, MATS, 2, TILE, TILE), BF),
    ]
    bufs += [pltpu.VMEM((3, g[1], 2, 32, TILE), BF) for g in GROUPS]
    bufs += [pltpu.VMEM((4, g[1], 16, TILE), F32) for g in GROUPS]
    bufs += [pltpu.VMEM((3, g[1], 16, TILE), F32) for g in GROUPS]
    bufs += [pltpu.VMEM((4, g[1], 16, TILE), F32) for g in GROUPS]
    sems = [
        pltpu.SemaphoreType.DMA((5, n)),
        pltpu.SemaphoreType.DMA((5, n)),
        pltpu.SemaphoreType.DMA((5, n, 3)),
        pltpu.SemaphoreType.DMA((5, n, 3)),
    ]
    return bufs, sems


def split_ar(refs):
    n = len(GROUPS)
    bufs = (*refs[:4], refs[4 : 4 + n], refs[4 + n : 4 + 2 * n], refs[4 + 2 * n : 4 + 3 * n], refs[4 + 3 * n : 4 + 4 * n])
    return bufs, refs[4 + 4 * n :]


def body(
    x_in, cot_in, cw_in, cb_in, dw_in, td_in, tu_in, cd_in, cu_in, live_in,
    gi_out, sums_out,
    xs, cext, cw, cb, dw, tiles, vown, send_l, send_r, recv_l, recv_r, big, mask,
    wcat, cwt, ht, xt, ab, feats, gps, gacc, cacc, bacc, gi, cd, cu, live_at,
    load_sem, store_sem, tile_send, tile_recv, pass_send, pass_recv, halo_send, halo_recv, *ar_refs,
):
    b, e, core, pos = place()
    right, left = ((b + 1) % 16, e), ((b + 15) % 16, e)
    sib = (b + 1 - 2 * core, e)
    barrier = pltpu.get_barrier_semaphore()
    greeted = [left, right] + [
        peer(core, pos, {axis: (pos[axis] + k) % 4}) for axis in ("x", "y", "z") for k in (1, 2, 3)
    ]
    for to in greeted:
        pl.semaphore_signal(barrier, inc=1, device_id=to, device_id_type=MESH)
    loads = [
        pltpu.make_async_copy(src, dst, load_sem.at[i])
        for i, (src, dst) in enumerate(
            [
                (live_in, live_at),
                (cd_in, cd),
                (cu_in, cu),
                (td_in, tiles.at[0]),
                (tu_in, tiles.at[1]),
                (x_in, xs),
                (cw_in, cw),
                (cb_in, cb),
                (cot_in, cext.at[:, 2 * TILE : 2 * TILE + ROWS, :]),
                (dw_in, dw),
            ]
        )
    ]
    for load in loads:
        load.start()

    loads[0].wait()
    live = live_at[0]
    reach = lax.broadcasted_iota(jnp.int32, (ROWS, CH), 0)
    mask[...] = jnp.where((reach < live - TILE) | (reach >= ROWS - TILE), 1.0, 0.0).astype(F32)
    for load in loads[1:5]:
        load.wait()
    for way, cols in enumerate((cd, cu)):
        for r in range(NB):
            keep = mask[r * TILE : (r + 1) * TILE, :TILE]
            slots = [tiles[way, r, k].astype(F32) for k in range(4)]
            for o in range(3):
                total = jnp.zeros((TILE, TILE), F32)
                if o == 0:
                    total = total + slots[0]
                if o == 2:
                    total = total + slots[1]
                for k in (2, 3):
                    total = total + jnp.where(cols[r, k] - r == o, 1.0, 0.0).astype(F32) * slots[k]
                total = total * keep
                if r == 0 and o == 0:
                    total = total * jnp.where(b > 0, 1.0, 0.0).astype(F32)
                if r == NB - 1 and o == 2:
                    total = total * jnp.where(b < 15, 1.0, 0.0).astype(F32)
                tile = total.T.astype(BF)
                vown[way, r, o] = tile
                if (r, o) in ((1, 2), (2, 1), (2, 2)):
                    send_r[way, ((1, 2), (2, 1), (2, 2)).index((r, o))] = tile
                if (r, o) in ((0, 0), (0, 1), (1, 0)):
                    send_l[way, ((0, 0), (0, 1), (1, 0)).index((r, o))] = tile

    pl.semaphore_wait(barrier, len(greeted))

    def halo(t):
        return [
            remote(
                cot_in.at[t, TILE:ROWS, :], cext.at[t, 0 : 2 * TILE, :],
                halo_send.at[t, 0], halo_recv.at[t, 0], right,
            ),
            remote(
                cot_in.at[t, 0 : 2 * TILE, :], cext.at[t, 2 * TILE + ROWS : EXT, :],
                halo_send.at[t, 1], halo_recv.at[t, 1], left,
            ),
        ]

    def halo_start(t):
        for copy in halo(t):
            copy.start()

    own = rows_at(pos["z"], 32)
    tile_copies = [
        remote(src.at[:, :, own, :], dst.at[:, :, own, :], tile_send.at[i], tile_recv.at[i], to)
        for i, (src, dst, to) in enumerate([(send_r, recv_l, right), (send_l, recv_r, left)])
    ]
    for copy in tile_copies:
        copy.start()
    halo_start(0)

    for load in loads[5:]:
        load.wait()

    def forward(t):
        pre = dot(xs[t], cw[0]) + dot(xs[t + STEP], cw[1]) + cb[...]
        f = jnp.tanh(pre[:, :CH])
        s = 0.5 * jnp.tanh(0.5 * pre[:, CH:]) + 0.5
        sm = s * mask[...]
        fs = f * sm
        ht[t] = fs.astype(BF).T
        ab[t, :, :CH] = sm * (1.0 - f * f)
        ab[t, :, CH:] = fs * (1.0 - s)

    pl.loop(0, T_OUT)(forward)
    passes = []
    for i, ref in enumerate((recv_l, recv_r)):
        tile_copies[i].wait()
        for k in (1, 2, 3):
            args = (pass_send.at[i, k - 1], pass_recv.at[i, k - 1], peer(core, pos, {"z": (pos["z"] + k) % 4}))
            theirs = rows_at((pos["z"] + 4 - k) % 4, 32)
            out = remote(ref.at[:, :, own, :], ref.at[:, :, own, :], *args)
            out.start()
            passes.append((out, remote(ref.at[:, :, own, :], ref.at[:, :, theirs, :], *args)))
    halo_start(1)
    halo_start(2)

    @pl.loop(0, T_IN)
    def _(t):
        xt[t] = xs[t].T

    for k in range(5):
        wcat[k * CH : (k + 1) * CH, :] = dw[k].T
    for k in range(2):
        cwt[k] = cw[k].T
    gacc[...] = jnp.zeros_like(gacc)
    cacc[...] = jnp.zeros_like(cacc)
    bacc[...] = jnp.zeros_like(bacc)

    for out, back in passes:
        back.wait_recv()
        out.wait_send()

    def v(way, i, k):
        if 0 <= i < NB:
            return vown[way, i, k - i + 1]
        if i < 0:
            return recv_l[way, ((-2, -1), (-1, -1), (-1, 0)).index((i, k))]
        return recv_r[way, ((3, 2), (3, 3), (4, 3)).index((i, k))]

    for j in range(NB):
        for way in range(2):
            for at, i in enumerate(range(j - 2, j + 3)):
                total = jnp.zeros((TILE, TILE), F32)
                for k in range(j - 1, j + 2):
                    if abs(i - k) <= 1:
                        total = total + dot(v(way, k, j), v(way, i, k))
                first = v(way, i, j) if abs(i - j) <= 1 else jnp.zeros((TILE, TILE), BF)
                big[j, way * TILE : (way + 1) * TILE, at * TILE : (at + 1) * TILE] = first
                big[j, (2 + way) * TILE : (3 + way) * TILE, at * TILE : (at + 1) * TILE] = total.astype(BF)

    def diffuse(t):
        for copy in halo(t):
            copy.wait_recv()
        if not isinstance(t, int):
            pl.when(t + 3 < T_OUT)(lambda: halo_start(t + 3))
        feats[:, :CH] = cext[t, 2 * TILE : 2 * TILE + ROWS, :]
        for j in range(NB):
            out = dot(big[j], cext[t, j * TILE : (j + 5) * TILE, :]).astype(BF)
            for at, k in enumerate((1, 3, 2, 4)):
                feats[j * TILE : (j + 1) * TILE, k * CH : (k + 1) * CH] = out[at * TILE : (at + 1) * TILE]
        gacc[...] += dot(ht[t], feats[...])

    def backward(t):
        gh = dot(feats[...], wcat[...])
        ga = gh * ab[t, :, :CH]
        gb = gh * ab[t, :, CH:]
        gp = jnp.concatenate([ga, gb], axis=1).astype(BF)
        gps[t] = gp
        cacc[...] += dot(jnp.concatenate([xt[t], xt[t + STEP]], axis=0), gp).reshape(2, CH, 2 * CH)
        bacc[...] += jnp.sum(gp.astype(F32).reshape(ROWS // 8, 8, 2 * CH), axis=0)

    @pl.loop(0, T_OUT - 1)
    def _(t):
        diffuse(t)
        backward(t)

    def half_of(m, c, half):
        if m < 5:
            return gacc[rows_at(half, TILE), m * CH + c * TILE : m * CH + (c + 1) * TILE]
        if m < 9:
            at = ((m - 5) % 2) * CH + c * TILE
            return cacc[(m - 5) // 2, rows_at(half, TILE), at : at + TILE]
        line = jnp.sum(bacc[...], axis=0, keepdims=True)
        row = lax.broadcasted_iota(jnp.int32, (16, TILE), 0)
        bias = jnp.zeros((16, TILE), F32)
        for i in range(4):
            part = jnp.broadcast_to(line[:, i * TILE : (i + 1) * TILE], (16, TILE))
            bias = bias + jnp.where(row == i, part, 0.0)
        return jnp.broadcast_to(bias[None], (TILE // 16, 16, TILE)).reshape(TILE, TILE)

    stores = []

    def inputs_grad(t):
        total = jnp.zeros((ROWS, CH), F32)
        if t < T_OUT:
            total = total + dot(gps[t], cwt[0])
        if t >= STEP:
            own_cot = cext[t - STEP, 2 * TILE : 2 * TILE + ROWS, :].astype(F32)
            total = total + dot(gps[t - STEP], cwt[1]) + own_cot * mask[...]
        gi[t] = total.astype(BF)
        store = pltpu.make_async_copy(gi.at[t], gi_out.at[t], store_sem.at[t])
        store.start()
        stores.append(store)

    bufs, sems = split_ar(ar_refs)
    reduce = AllReduce(half_of, core, pos, sib, bufs, sems)
    groups = range(len(GROUPS))
    diffuse(T_OUT - 1)
    reduce.core_send(0)
    backward(T_OUT - 1)
    for g in groups[1:]:
        reduce.core_send(g)
    for stage, steps in (
        (reduce.scatter_first, (0, 1)),
        (reduce.scatter_second, (2, 3)),
        (reduce.sum_third, (4, 5)),
        (reduce.gather_second, (6, 7)),
        (reduce.gather_first, ()),
        (reduce.gather_core, ()),
        (reduce.end, ()),
    ):
        for g in groups:
            stage(g)
        for t in steps:
            inputs_grad(t)
    last = pltpu.make_async_copy(bufs[3], sums_out, store_sem.at[T_IN])
    last.start()
    for t in range(T_OUT):
        for copy in halo(t):
            copy.wait_send()
    for g in groups:
        reduce.drain(g)
    for store in stores:
        store.wait()
    last.wait()


def unpack(scale, gi_in, sums_in, gi_out, gc_out, gb_out, gd_out, gi, sums, gc, gd, sem):
    first = pltpu.make_async_copy(sums_in, sums, sem.at[0, T_IN])
    ins = [pltpu.make_async_copy(gi_in.at[t], gi.at[t], sem.at[0, t]) for t in range(T_IN)]
    outs = [pltpu.make_async_copy(gi.at[t], gi_out.at[t], sem.at[1, t]) for t in range(T_IN)]
    first.start()
    for copy in ins:
        copy.start()
    first.wait()
    for copy, out in zip(ins, outs):
        copy.wait()
        out.start()
    for m in range(9):
        for h in range(2):
            for c in range(2):
                rows = slice(h * TILE, (h + 1) * TILE)
                part = sums[h, m, c].astype(F32) * scale
                if m < 5:
                    gd[m, rows, c * TILE : (c + 1) * TILE] = part
                else:
                    at = ((m - 5) % 2) * CH + c * TILE
                    gc[(m - 5) // 2, rows, at : at + TILE] = part
        if m == 4:
            outs.append(pltpu.make_async_copy(gd, gd_out, sem.at[1, T_IN]))
            outs[-1].start()
    outs.append(pltpu.make_async_copy(gc, gc_out, sem.at[1, T_IN + 1]))
    outs[-1].start()
    bias = sums[0, 9, 0, 0:16, :].astype(F32) * scale
    for i in range(4):
        gb_out[:, i * TILE : (i + 1) * TILE] = bias[i : i + 1]
    for out in outs:
        out.wait()


def on_device(x, cot, cw, cb, dw, td, tu, cd, cu, live):
    scale = float(8 * T_OUT * 6144) ** (-0.5)
    bufs, sems = ar_scratch()
    anywhere = pl.BlockSpec(memory_space=pl.ANY)
    vmem = pl.BlockSpec(memory_space=pltpu.VMEM)
    gi, sums = pl.pallas_call(
        body,
        out_shape=(
            jax.ShapeDtypeStruct((T_IN, ROWS, CH), BF),
            jax.ShapeDtypeStruct((2, MATS, 2, TILE, TILE), BF),
        ),
        in_specs=[anywhere] * 10,
        out_specs=(anywhere,) * 2,
        scratch_shapes=[
            pltpu.VMEM((T_IN, ROWS, CH), BF),
            pltpu.VMEM((T_OUT, EXT, CH), BF),
            pltpu.VMEM((2, CH, 2 * CH), BF),
            pltpu.VMEM((1, 2 * CH), F32),
            pltpu.VMEM((5, CH, CH), BF),
            pltpu.VMEM((2, NB, 4, TILE, TILE), BF),
            pltpu.VMEM((2, NB, 3, TILE, TILE), BF),
            pltpu.VMEM((2, 3, TILE, TILE), BF),
            pltpu.VMEM((2, 3, TILE, TILE), BF),
            pltpu.VMEM((2, 3, TILE, TILE), BF),
            pltpu.VMEM((2, 3, TILE, TILE), BF),
            pltpu.VMEM((NB, 4 * TILE, 5 * TILE), BF),
            pltpu.VMEM((ROWS, CH), F32),
            pltpu.VMEM((5 * CH, CH), BF),
            pltpu.VMEM((2, 2 * CH, CH), BF),
            pltpu.VMEM((T_OUT, CH, ROWS), BF),
            pltpu.VMEM((T_IN, CH, ROWS), BF),
            pltpu.VMEM((T_OUT, ROWS, 2 * CH), F32),
            pltpu.VMEM((ROWS, 5 * CH), BF),
            pltpu.VMEM((T_OUT, ROWS, 2 * CH), BF),
            pltpu.VMEM((CH, 5 * CH), F32),
            pltpu.VMEM((2, CH, 2 * CH), F32),
            pltpu.VMEM((8, 2 * CH), F32),
            pltpu.VMEM((T_IN, ROWS, CH), BF),
            pltpu.SMEM((NB, 4), jnp.int32),
            pltpu.SMEM((NB, 4), jnp.int32),
            pltpu.SMEM((1,), jnp.int32),
            pltpu.SemaphoreType.DMA((10,)),
            pltpu.SemaphoreType.DMA((T_IN + 1,)),
            pltpu.SemaphoreType.DMA((2,)),
            pltpu.SemaphoreType.DMA((2,)),
            pltpu.SemaphoreType.DMA((2, 3)),
            pltpu.SemaphoreType.DMA((2, 3)),
            pltpu.SemaphoreType.DMA((T_OUT, 2)),
            pltpu.SemaphoreType.DMA((T_OUT, 2)),
            *bufs,
            *sems,
        ],
        compiler_params=pltpu.CompilerParams(
            collective_id=0, has_side_effects=True, vmem_limit_bytes=61 << 20
        ),
    )(x[0], cot[0], cw, cb.reshape(1, -1), dw, td, tu, cd, cu, live)
    gi, gc, gb, gd = pl.pallas_call(
        functools.partial(unpack, scale),
        out_shape=(
            jax.ShapeDtypeStruct((T_IN, ROWS, CH), BF),
            jax.ShapeDtypeStruct((2, CH, 2 * CH), F32),
            jax.ShapeDtypeStruct((1, 2 * CH), F32),
            jax.ShapeDtypeStruct((5, CH, CH), F32),
        ),
        in_specs=[anywhere] * 2,
        out_specs=(anywhere, anywhere, vmem, anywhere),
        scratch_shapes=[
            pltpu.VMEM((T_IN, ROWS, CH), BF),
            pltpu.VMEM((2, MATS, 2, TILE, TILE), BF),
            pltpu.VMEM((2, CH, 2 * CH), F32),
            pltpu.VMEM((5, CH, CH), F32),
            pltpu.SemaphoreType.DMA((2, T_IN + 2)),
        ],
        compiler_params=pltpu.CompilerParams(vmem_limit_bytes=61 << 20),
    )(gi, sums)
    return gi[None], gc, gb.reshape(-1), gd


def solution(mesh):
    return jax.shard_map(
        on_device,
        mesh=mesh,
        in_specs=(
            P("event", None, "basin", None),
            P("event", None, "basin", None),
            P(),
            P(),
            P(),
            P("basin", None, None, None),
            P("basin", None, None, None),
            P("basin", None),
            P("basin", None),
            P("basin"),
        ),
        out_specs=(P("event", None, "basin", None), P(), P(), P()),
        check_vma=False,
    )
```
